32 devices in a mesh: groups: 2 (over y), ctx: 4 (over z), stream: 2 (over x), head: 2 (over core).
Axes of the slice: x: 2, y: 2, z: 4, core: 2. Of those that a mesh axis runs over, the one named last changes fastest.
Arguments:
- queries: bfloat16 [4, 2048, 12, 128], P(('groups', 'stream'), 'ctx', 'head'), parts along dimension 0, may hold values from -9 to 9
- new_keys: bfloat16 [4, 2048, 4, 128], P(('groups', 'stream'), 'ctx', 'head'), parts along dimension 0, may hold values from -4 to 4
- new_values: bfloat16 [4, 2048, 4, 128], P(('groups', 'stream'), 'ctx', 'head'), parts along dimension 0, may hold values from -6 to 6
- cache_keys: bfloat16 [4, 6144, 4, 128], P(('groups', 'stream'), 'ctx', 'head'), parts along dimension 0, may hold values from -6 to 6
- cache_values: bfloat16 [4, 6144, 4, 128], P(('groups', 'stream'), 'ctx', 'head'), parts along dimension 0, may hold values from -6 to 6
- block_slot: int32 [4, 48], P(('groups', 'stream')), parts along dimension 0, may hold values from 0 to 47, as said below
- block_lists: int32 [4, 4, 4, 32], P(('groups', 'stream'), 'head'), parts along dimension 0, may hold values from 0 to 47, as said below
- frame_pos: int32 [4], P(('groups', 'stream')), parts along dimension 0, may hold values from 4609 to 6144, as said below
Outputs:
- attended: bfloat16 [4, 2048, 12, 128], P(('groups', 'stream'), 'ctx', 'head'), parts along dimension 0
The draws below stay inside these ranges and needn't reach their ends.
There are 2 independent parts, one for each index of `groups`. The reference program is written for one: setup_inputs(seed, part) draws one part's arguments, and reference() takes and returns one part's arrays. A program takes and returns all parts, laid end to end along the dimension named above; each array names one. Nothing has to cross between parts.
Inputs may be any that keep to these rules, and one draw needn't show every extreme that they name: `block_slot`: each stream's row names every slot once; slot j lies on index j // 12 of ctx; logical blocks whose numbers agree modulo 48 / 12 lie on one index of ctx, and blocks of different residues on different indices. `block_lists`: each list holds 32 distinct logical blocks: first the 4 most recent blocks that hold cached tokens of the stream, ascending, the last being the block of position frame_pos - 1; then 28 older blocks. At most 8 blocks of a list lie on one index of ctx, and exactly 8 on the index that holds the list's last recent block. `frame_pos`: stream 0 has a full cache.
All inputs are finite; a program needn't handle non-finite values.
Results may differ from the reference program's by a relative error of at most 0.015.
Values may be sent and summed in bfloat16 or wider, within the bound.
A program may use at most 192 MiB of HBM per device.

```python
import jax
import jax.numpy as jnp
from jax import lax

QH = 12
KVH = 4
HD = 128
BLOCK = 128
RECENT = 4
SPARSE = 28
FRAME = 2048
CB_DEV = 12
TOK_DEV = 512
STREAMS = 2
TILES = 4
NB = 48
CACHE = 6144
MOST = 8


def layout(key):
    key = jax.random.fold_in(key, 5)
    subkeys = jax.random.split(key, 6)
    ranks_count = NB // CB_DEV
    filled = CACHE - jax.random.randint(subkeys[0], (STREAMS,), 0, CACHE // 4)
    filled = filled.at[0].set(CACHE).astype(jnp.int32)
    residues = jnp.arange(ranks_count, dtype=jnp.int32)
    owner_scores = jax.random.randint(subkeys[1], (STREAMS, ranks_count), 0, 1 << 20) * ranks_count + residues
    owner_of_residue = jnp.argsort(owner_scores, axis=-1).astype(jnp.int32)
    residue_of_owner = jnp.argsort(owner_of_residue, axis=-1).astype(jnp.int32)
    places = jnp.arange(CB_DEV, dtype=jnp.int32)
    local_scores = jax.random.randint(subkeys[2], (STREAMS, ranks_count, CB_DEV), 0, 1 << 20) * CB_DEV + places
    local_order = jnp.argsort(local_scores, axis=-1).astype(jnp.int32)
    block_ids = jnp.arange(NB, dtype=jnp.int32)
    stream_rows = jnp.arange(STREAMS, dtype=jnp.int32)[:, None]
    block_owner = owner_of_residue[stream_rows, (block_ids % ranks_count)[None, :]]
    within = (block_ids // ranks_count)[None, :]
    slot_table = (block_owner * CB_DEV + local_order[stream_rows, block_owner, within]).astype(jnp.int32)
    newest = (filled - 1) // BLOCK
    older_count = newest - RECENT + 1
    recent = newest[:, None] - RECENT + 1 + jnp.arange(RECENT, dtype=jnp.int32)[None, :]
    recent_owner = owner_of_residue[stream_rows, recent % ranks_count]
    newest_owner = recent_owner[:, -1]
    owner_ids = jnp.arange(ranks_count, dtype=jnp.int32)
    taken_count = jnp.sum((recent_owner[:, :, None] == owner_ids[None, None, :]).astype(jnp.int32), axis=1)
    spare_room = MOST - taken_count
    cell_ids = jnp.arange(ranks_count * MOST, dtype=jnp.int32)
    cell_owner = cell_ids // MOST
    cell_rank = cell_ids % MOST
    allowed_cell = cell_rank[None, :] < spare_room[:, cell_owner]
    newest_cell = cell_owner[None, :] == newest_owner[:, None]
    jitter = jax.random.randint(subkeys[3], (STREAMS, KVH, TILES, ranks_count * MOST), 0, 1 << 20)
    priority = jnp.where(newest_cell[:, None, None, :], 0, 1 + jitter)
    priority = jnp.where(allowed_cell[:, None, None, :], priority, 1 << 21)
    priority = priority * (ranks_count * MOST) + cell_ids
    picked = jnp.argsort(priority, axis=-1)[..., :SPARSE].astype(jnp.int32)
    shuffle_scores = jax.random.randint(subkeys[4], (STREAMS, KVH, TILES, SPARSE), 0, 1 << 20) * SPARSE
    shuffle = jnp.argsort(shuffle_scores + jnp.arange(SPARSE, dtype=jnp.int32), axis=-1)
    picked = jnp.take_along_axis(picked, shuffle, axis=-1)
    pick_owner = picked // MOST
    pick_rank = picked % MOST
    stream_four = jnp.arange(STREAMS, dtype=jnp.int32)[:, None, None, None]
    pick_residue = residue_of_owner[stream_four, pick_owner]
    class_count = (older_count[:, None, None, None] - pick_residue + ranks_count - 1) // ranks_count
    base_pick = jax.random.randint(subkeys[5], (STREAMS, KVH, TILES, ranks_count), 0, 1 << 20)
    first_pick = jnp.take_along_axis(base_pick, pick_owner, axis=-1) % class_count
    stride_pick = (first_pick + pick_rank) % class_count
    older_ids = (pick_residue + ranks_count * stride_pick).astype(jnp.int32)
    recent_all = jnp.broadcast_to(recent[:, None, None, :], (STREAMS, KVH, TILES, RECENT)).astype(jnp.int32)
    return (filled, slot_table, jnp.concatenate([recent_all, older_ids], axis=-1).astype(jnp.int32))


def draw_frame_pos(key, part):
    filled, slot_table, chosen = layout(key)
    return filled


def draw_block_slot(key, part):
    filled, slot_table, chosen = layout(key)
    return slot_table


def draw_block_lists(key, part):
    filled, slot_table, chosen = layout(key)
    return chosen


def draw_queries(key, part):
    key = jax.random.fold_in(key, 11)
    values = jnp.clip(jax.random.normal(key, (STREAMS, FRAME, QH, HD)), -4.0, 4.0)
    return values.astype(jnp.bfloat16)


def draw_new_keys(key, part):
    key = jax.random.fold_in(key, 23)
    values = jnp.clip(jax.random.normal(key, (STREAMS, FRAME, KVH, HD)), -4.0, 4.0)
    return values.astype(jnp.bfloat16)


def block_scale(key, shape, cuts, least, top_value):
    gain = 1.0
    for position, blocks in cuts:
        steps = jax.random.uniform(jax.random.fold_in(jax.random.fold_in(key, 6), position), (blocks,), jnp.float32, least / len(cuts), top_value / len(cuts))
        gain = gain * jnp.repeat(jnp.exp(steps), shape[position] // blocks).reshape((-1,) + (1,) * (len(shape) - 1 - position))
    return gain


def gaussian(stream_key, shape, width, most, pieces=(), kind=jnp.bfloat16):
    gain = block_scale(stream_key, shape, pieces, -0.22, 0.18) if pieces else 1.0
    values = jax.random.normal(stream_key, shape, jnp.float32) * width * gain
    return jnp.minimum(jnp.maximum(values, -most), most).astype(kind)


def setup_inputs(seed: int = 0, part: int = 0) -> dict:
    key_of = jax.random.split(jax.random.key(seed), 9)
    part_splits = jax.random.split(jax.random.fold_in(key_of[8], part), 9)
    return {
        "queries": draw_queries(jax.random.fold_in(jax.random.fold_in(key_of[8], part), 71), part),
        "new_keys": draw_new_keys(jax.random.fold_in(jax.random.fold_in(key_of[8], part), 71), part),
        "new_values": gaussian(part_splits[2], (STREAMS, FRAME, KVH, HD), 1.0, 6.0, ((0, 2), (1, 4), (2, 2))),
        "cache_keys": gaussian(part_splits[3], (STREAMS, CACHE, KVH, HD), 1.0, 6.0, ((0, 2), (1, 4), (2, 2))),
        "cache_values": gaussian(part_splits[4], (STREAMS, CACHE, KVH, HD), 1.0, 6.0, ((0, 2), (1, 4), (2, 2))),
        "block_slot": draw_block_slot(jax.random.fold_in(jax.random.fold_in(key_of[8], part), 71), part),
        "block_lists": draw_block_lists(jax.random.fold_in(jax.random.fold_in(key_of[8], part), 71), part),
        "frame_pos": draw_frame_pos(jax.random.fold_in(jax.random.fold_in(key_of[8], part), 71), part),
    }


def reference(queries, new_keys, new_values, cache_keys, cache_values, block_slot, block_lists, frame_pos):
    group_size = QH // KVH
    scale = HD ** -0.5
    offsets = jnp.arange(BLOCK, dtype=jnp.int32)

    def one_head(indices):
        stream_idx, kv_index = indices
        query_rows = lax.dynamic_slice_in_dim(queries[stream_idx], kv_index * group_size, group_size, 1)
        query_rows = query_rows.astype(jnp.float32).reshape(TILES, TOK_DEV, group_size, HD)
        key_new = new_keys[stream_idx][:, kv_index].astype(jnp.float32)
        value_new = new_values[stream_idx][:, kv_index].astype(jnp.float32)
        chosen = block_lists[stream_idx, kv_index]
        stored = block_slot[stream_idx][chosen]
        row_ids = (stored[..., None] * BLOCK + offsets).astype(jnp.int32)
        usable = (chosen[..., None] * BLOCK + offsets) < frame_pos[stream_idx]
        key_old = cache_keys[stream_idx][:, kv_index][row_ids].astype(jnp.float32)
        value_old = cache_values[stream_idx][:, kv_index][row_ids].astype(jnp.float32)
        score_new = jnp.einsum('tngd,kd->tngk', query_rows, key_new) * scale
        score_old = jnp.einsum('tngd,tlbd->tnglb', query_rows, key_old) * scale
        masked = usable[:, None, None]
        score_old = jnp.where(masked, score_old, -1e30)
        peak = jnp.maximum(score_new.max(-1), score_old.max((-2, -1)))
        weight_new = jnp.exp(score_new - peak[..., None])
        weight_old = jnp.where(masked, jnp.exp(score_old - peak[..., None, None]), 0.0)
        totals = weight_new.sum(-1) + weight_old.sum((-2, -1))
        rounded_new = lax.optimization_barrier(weight_new.astype(jnp.bfloat16)).astype(jnp.float32)
        rounded_old = lax.optimization_barrier(weight_old.astype(jnp.bfloat16)).astype(jnp.float32)
        summed = jnp.einsum('tngk,kd->tngd', rounded_new, value_new)
        summed = summed + jnp.einsum('tnglb,tlbd->tngd', rounded_old, value_old)
        result = (summed / totals[..., None]).astype(jnp.bfloat16)
        return result.reshape(FRAME, group_size, HD)

    stream_ids = jnp.repeat(jnp.arange(STREAMS, dtype=jnp.int32), KVH)
    head_ids = jnp.tile(jnp.arange(KVH, dtype=jnp.int32), STREAMS)
    outputs = lax.map(one_head, (stream_ids, head_ids))
    outputs = outputs.reshape(STREAMS, KVH, FRAME, group_size, HD).transpose(0, 2, 1, 3, 4)
    return outputs.reshape(STREAMS, FRAME, QH, HD)
```

```python
import functools

import jax
import jax.numpy as jnp
from jax import lax
from jax.experimental import pallas as pl
from jax.experimental.pallas import tpu as pltpu
from jax.sharding import PartitionSpec as P

BLOCK = 128
FLOOR = -1e30
LOG2E = 1.4426950408889634
MESH = pl.DeviceIdType.MESH


def lookup(slot_table, indices):
    entries = jnp.arange(slot_table.shape[0], dtype=jnp.int32)
    return jnp.sum(jnp.where(indices[..., None] == entries, slot_table, 0), axis=-1)


def local_blocks(slot_table, lists, filled, own_index, cb_dev, capacity):
    slot_entry = lookup(slot_table, lists)
    mine = (slot_entry // cb_dev) == own_index
    count = lists.shape[-1]
    positions = jnp.arange(count, dtype=jnp.int32)
    earlier = positions[:, None] > positions[None, :]
    rank = jnp.sum((mine[..., None, :] & earlier).astype(jnp.int32), axis=-1)
    slot_ids = jnp.arange(capacity, dtype=jnp.int32)
    matched = mine[..., None] & (rank[..., None] == slot_ids)
    rows = jnp.clip(filled - lists * BLOCK, 0, BLOCK)
    slots = jnp.sum(jnp.where(matched, (slot_entry % cb_dev)[..., None], 0), axis=2)
    limits = jnp.sum(jnp.where(matched, rows[..., None], 0), axis=2)
    return slots, limits


def kernel(
    n, slots_ref, limits_ref, q_ref, kn_ref, vn_ref, kc_ref, vc_ref, out_ref,
    qbuf, rin, lin, rout, lout, acc, lacc, qs, qr, rs, rr, ls, lr,
):
    heads, tok, hd = q_ref.shape
    group = heads // kn_ref.shape[0]
    capacity = slots_ref.shape[2]
    me = lax.axis_index("ctx")
    scale = LOG2E * hd ** -0.5

    barrier = pltpu.get_barrier_semaphore()

    @pl.when(me > 0)
    def _():
        pl.semaphore_signal(barrier, inc=1, device_id={"ctx": me - 1}, device_id_type=MESH)

    @pl.when(me < n - 1)
    def _():
        pl.semaphore_signal(barrier, inc=1, device_id={"ctx": me + 1}, device_id_type=MESH)

    peers = jnp.where(me > 0, 1, 0) + jnp.where(me < n - 1, 1, 0)
    pl.semaphore_wait(barrier, peers)

    def q_copy(src, way, t, h):
        return pltpu.make_async_remote_copy(
            src_ref=src, dst_ref=qbuf.at[t, h], send_sem=qs.at[way, t, h], recv_sem=qr.at[t, h],
            device_id={"ctx": me + 1 - 2 * way}, device_id_type=MESH,
        )

    def r_copies(way, t, h):
        peer = {"ctx": me + 1 - 2 * way}
        return (
            pltpu.make_async_remote_copy(
                src_ref=rout.at[t, h], dst_ref=rin.at[way, t, h], send_sem=rs.at[t, h],
                recv_sem=rr.at[way, t, h], device_id=peer, device_id_type=MESH,
            ),
            pltpu.make_async_remote_copy(
                src_ref=lout.at[t, h], dst_ref=lin.at[way, t, h], send_sem=ls.at[t, h],
                recv_sem=lr.at[way, t, h], device_id=peer, device_id_type=MESH,
            ),
        )

    def can_send(way):
        return me < n - 1 if way == 0 else me > 0

    @pl.loop(0, heads)
    def _(h):
        for way in (0, 1):
            @pl.when(can_send(way))
            def _():
                q_copy(q_ref.at[h], way, me, h).start()

    def partial(q, t, h):
        g = h // group
        rows = lax.broadcasted_iota(jnp.int32, (BLOCK, tok), 0)
        nt = (((1,), (1,)), ((), ()))
        pieces = [
            ([lax.dot_general(kn_ref[g], q, nt, preferred_element_type=jnp.float32)], vn_ref[g])
        ]
        for first in range(0, capacity, 4):
            ids = range(first, min(first + 4, capacity))
            where = [slots_ref[g, t, c] for c in ids]
            keys = jnp.concatenate([kc_ref[g, w] for w in where], axis=0)
            values = jnp.concatenate([vc_ref[g, w] for w in where], axis=1)
            s = lax.dot_general(keys, q, nt, preferred_element_type=jnp.float32)
            parts = []
            for k, c in enumerate(ids):
                block = s[k * BLOCK:(k + 1) * BLOCK]
                parts.append(jnp.where(rows < limits_ref[g, t, c], block, FLOOR))
            pieces.append((parts, values))
        peak = None
        for parts, _ in pieces:
            for s in parts:
                top = jnp.max(s, axis=0, keepdims=True)
                peak = top if peak is None else jnp.maximum(peak, top)
        peak = peak * scale
        total = jnp.zeros((1, tok), jnp.float32)
        running = jnp.zeros((hd, tok), jnp.float32)
        for parts, values in pieces:
            weights = []
            for s in parts:
                w = jnp.exp2(s * scale - peak)
                total = total + jnp.sum(w, axis=0, keepdims=True)
                weights.append(w.astype(jnp.bfloat16))
            p = weights[0] if len(weights) == 1 else jnp.concatenate(weights, axis=0)
            running = running + jnp.dot(values, p, preferred_element_type=jnp.float32)
        return running / total, peak + jnp.log2(total)

    def merge(way, t, h):
        theirs, ours = lin[way, t, h], lacc[t, h]
        top = jnp.maximum(theirs, ours)
        a, b = jnp.exp2(theirs - top), jnp.exp2(ours - top)
        both = a + b
        mixed = rin[way, t, h].astype(jnp.float32) * (a / both) + acc[t, h] * (b / both)
        return mixed, top + jnp.log2(both)

    def emit(way, t, h, o, l):
        rout[t, h] = o.astype(jnp.bfloat16)
        lout[t, h] = l
        for copy in r_copies(way, t, h):
            copy.start()

    @pl.loop(0, heads)
    def _(h):
        o, l = partial(q_ref[h], me, h)
        acc[me, h] = o
        lacc[me, h] = l

    @pl.loop(1, n)
    def _(r):
        @pl.loop(0, heads)
        def _(h):
            for way in (0, 1):
                t = me - r if way == 0 else me + r
                there = t >= 0 if way == 0 else t < n

                @pl.when(there)
                def _():
                    q_copy(qbuf.at[t, h], way, t, h).wait_recv()

                    @pl.when(can_send(way))
                    def _():
                        q_copy(qbuf.at[t, h], way, t, h).start()

            for way in (0, 1):
                t = me - r if way == 0 else me + r
                there = t >= 0 if way == 0 else t < n

                @pl.when(there)
                def _():
                    o, l = partial(qbuf[t, h], t, h)

                    @pl.when(can_send(way))
                    def _():
                        acc[t, h] = o
                        lacc[t, h] = l

                    @pl.when(jnp.logical_not(can_send(way)))
                    def _():
                        emit(1 - way, t, h, o, l)

            for way in (0, 1):
                t = r if way == 0 else n - 1 - r
                inner = (me > 0) & (me < t) if way == 0 else (me < n - 1) & (me > t)

                @pl.when(inner)
                def _():
                    for copy in r_copies(way, t, h):
                        copy.wait_recv()
                    o, l = merge(way, t, h)
                    emit(way, t, h, o, l)

                @pl.when(me == t)
                def _():
                    for copy in r_copies(way, t, h):
                        copy.wait_recv()
                    o, l = merge(way, t, h)
                    acc[t, h] = o
                    lacc[t, h] = l

    @pl.loop(0, heads)
    def _(h):
        out_ref[h] = acc[me, h].T.astype(out_ref.dtype)
        for way in (0, 1):
            @pl.when(can_send(way))
            def _():
                q_copy(q_ref.at[h], way, me, h).wait_send()

        @pl.loop(0, n)
        def _(t):
            @pl.when(t != me)
            def _():
                for copy in r_copies(0, t, h):
                    copy.wait_send()

            @pl.when((t < me) & can_send(0))
            def _():
                q_copy(qbuf.at[t, h], 0, t, h).wait_send()

            @pl.when((t > me) & can_send(1))
            def _():
                q_copy(qbuf.at[t, h], 1, t, h).wait_send()


def shards(
    n, queries, new_keys, new_values, cache_keys, cache_values, block_slot, block_lists, frame_pos
):
    tok, heads, hd = queries.shape[1:]
    kv_heads = new_keys.shape[2]
    cb_dev = cache_keys.shape[1] // BLOCK
    capacity = min(cb_dev, max(2, -(-block_lists.shape[3] // n)))
    slots, limits = local_blocks(
        block_slot[0], block_lists[0], frame_pos[0], lax.axis_index("ctx"), cb_dev, capacity
    )
    q = jnp.transpose(queries[0], (1, 0, 2))
    kn = jnp.transpose(new_keys[0], (1, 0, 2))
    vn = jnp.transpose(new_values[0], (1, 2, 0))
    kc = jnp.transpose(cache_keys[0].reshape(cb_dev, BLOCK, kv_heads, hd), (2, 0, 1, 3))
    vc = jnp.transpose(cache_values[0].reshape(cb_dev, BLOCK, kv_heads, hd), (2, 0, 3, 1))
    smem = pl.BlockSpec(memory_space=pltpu.SMEM)
    vmem = pl.BlockSpec(memory_space=pltpu.VMEM)
    bf16, f32 = jnp.bfloat16, jnp.float32
    dma = pltpu.SemaphoreType.DMA
    out = pl.pallas_call(
        functools.partial(kernel, n),
        out_shape=jax.ShapeDtypeStruct((heads, tok, hd), bf16),
        in_specs=[smem, smem] + [vmem] * 5,
        out_specs=vmem,
        scratch_shapes=[
            pltpu.VMEM((n, heads, tok, hd), bf16),
            pltpu.VMEM((2, n, heads, hd, tok), bf16),
            pltpu.VMEM((2, n, heads, 1, tok), f32),
            pltpu.VMEM((n, heads, hd, tok), bf16),
            pltpu.VMEM((n, heads, 1, tok), f32),
            pltpu.VMEM((n, heads, hd, tok), f32),
            pltpu.VMEM((n, heads, 1, tok), f32),
            dma((2, n, heads)),
            dma((n, heads)),
            dma((n, heads)),
            dma((2, n, heads)),
            dma((n, heads)),
            dma((2, n, heads)),
        ],
        compiler_params=pltpu.CompilerParams(
            collective_id=0, has_side_effects=True, vmem_limit_bytes=56 * 1024 * 1024
        ),
    )(slots, limits, q, kn, vn, kc, vc)
    return jnp.transpose(out, (1, 0, 2))[None]


def solution(mesh):
    placed = (
        P(("groups", "stream"), "ctx", "head", None),
        P(("groups", "stream"), "ctx", "head", None),
        P(("groups", "stream"), "ctx", "head", None),
        P(("groups", "stream"), "ctx", "head", None),
        P(("groups", "stream"), "ctx", "head", None),
        P(("groups", "stream"), None),
        P(("groups", "stream"), "head", None, None),
        P(("groups", "stream")),
    )
    return jax.shard_map(
        functools.partial(shards, mesh.shape["ctx"]),
        mesh=mesh,
        in_specs=placed,
        out_specs=P(("groups", "stream"), "ctx", "head", None),
        check_vma=False,
    )
```

```python
import functools

import jax
import jax.numpy as jnp
from jax import lax
from jax.experimental import pallas as pl
from jax.experimental.pallas import tpu as pltpu
from jax.sharding import PartitionSpec as P

BLOCK = 128
FLOOR = -1e30
LOG2E = 1.4426950408889634
MESH = pl.DeviceIdType.MESH


def lookup(slot_table, indices):
    entries = jnp.arange(slot_table.shape[0], dtype=jnp.int32)
    return jnp.sum(jnp.where(indices[..., None] == entries, slot_table, 0), axis=-1)


def local_blocks(slot_table, lists, filled, own_index, cb_dev, capacity):
    slot_entry = lookup(slot_table, lists)
    mine = (slot_entry // cb_dev) == own_index
    count = lists.shape[-1]
    positions = jnp.arange(count, dtype=jnp.int32)
    earlier = positions[:, None] > positions[None, :]
    rank = jnp.sum((mine[..., None, :] & earlier).astype(jnp.int32), axis=-1)
    slot_ids = jnp.arange(capacity, dtype=jnp.int32)
    matched = mine[..., None] & (rank[..., None] == slot_ids)
    rows = jnp.clip(filled - lists * BLOCK, 0, BLOCK)
    slots = jnp.sum(jnp.where(matched, (slot_entry % cb_dev)[..., None], 0), axis=2)
    limits = jnp.sum(jnp.where(matched, rows[..., None], 0), axis=2)
    return slots, limits


def kernel(
    n, slots_ref, limits_ref, q_ref, kn_ref, vn_ref, kc_ref, vc_ref, out_ref,
    qbuf, rin, lin, rout, lout, acc, lacc, qs, qr, rs, rr, ls, lr,
):
    heads, tok, hd = q_ref.shape
    group = heads // kn_ref.shape[0]
    capacity = slots_ref.shape[2]
    me = lax.axis_index("ctx")
    scale = LOG2E * hd ** -0.5

    barrier = pltpu.get_barrier_semaphore()

    @pl.when(me > 0)
    def _():
        pl.semaphore_signal(barrier, inc=1, device_id={"ctx": me - 1}, device_id_type=MESH)

    @pl.when(me < n - 1)
    def _():
        pl.semaphore_signal(barrier, inc=1, device_id={"ctx": me + 1}, device_id_type=MESH)

    peers = jnp.where(me > 0, 1, 0) + jnp.where(me < n - 1, 1, 0)
    pl.semaphore_wait(barrier, peers)

    def q_copy(src, way, t, h):
        return pltpu.make_async_remote_copy(
            src_ref=src, dst_ref=qbuf.at[t, h], send_sem=qs.at[way, t, h], recv_sem=qr.at[t, h],
            device_id={"ctx": me + 1 - 2 * way}, device_id_type=MESH,
        )

    def r_copies(way, t, h):
        peer = {"ctx": me + 1 - 2 * way}
        return (
            pltpu.make_async_remote_copy(
                src_ref=rout.at[t, h], dst_ref=rin.at[way, t, h], send_sem=rs.at[t, h],
                recv_sem=rr.at[way, t, h], device_id=peer, device_id_type=MESH,
            ),
            pltpu.make_async_remote_copy(
                src_ref=lout.at[t, h], dst_ref=lin.at[way, t, h], send_sem=ls.at[t, h],
                recv_sem=lr.at[way, t, h], device_id=peer, device_id_type=MESH,
            ),
        )

    def can_send(way):
        return me < n - 1 if way == 0 else me > 0

    @pl.loop(0, heads)
    def _(h):
        for way in (0, 1):
            @pl.when(can_send(way))
            def _():
                q_copy(q_ref.at[h], way, me, h).start()

    def partial(q, t, h):
        g = h // group
        rows = lax.broadcasted_iota(jnp.int32, (BLOCK, tok), 0)
        nt = (((1,), (1,)), ((), ()))
        pieces = [
            ([lax.dot_general(kn_ref[g], q, nt, preferred_element_type=jnp.float32)], vn_ref[g])
        ]
        for first in range(0, capacity, 4):
            ids = range(first, min(first + 4, capacity))
            where = [slots_ref[g, t, c] for c in ids]
            keys = jnp.concatenate([kc_ref[g, w] for w in where], axis=0)
            values = jnp.concatenate([vc_ref[g, w] for w in where], axis=1)
            s = lax.dot_general(keys, q, nt, preferred_element_type=jnp.float32)
            parts = []
            for k, c in enumerate(ids):
                block = s[k * BLOCK:(k + 1) * BLOCK]
                parts.append(jnp.where(rows < limits_ref[g, t, c], block, FLOOR))
            pieces.append((parts, values))
        peak = None
        for parts, _ in pieces:
            for s in parts:
                top = jnp.max(s, axis=0, keepdims=True)
                peak = top if peak is None else jnp.maximum(peak, top)
        peak = peak * scale
        total = jnp.zeros((1, tok), jnp.float32)
        running = jnp.zeros((hd, tok), jnp.float32)
        for parts, values in pieces:
            weights = []
            for s in parts:
                w = jnp.exp2(s * scale - peak)
                total = total + jnp.sum(w, axis=0, keepdims=True)
                weights.append(w.astype(jnp.bfloat16))
            p = weights[0] if len(weights) == 1 else jnp.concatenate(weights, axis=0)
            running = running + jnp.dot(values, p, preferred_element_type=jnp.float32)
        return running / total, peak + jnp.log2(total)

    def merge(way, t, h):
        theirs, ours = lin[way, t, h], lacc[t, h]
        top = jnp.maximum(theirs, ours)
        a, b = jnp.exp2(theirs - top), jnp.exp2(ours - top)
        both = a + b
        mixed = rin[way, t, h].astype(jnp.float32) * (a / both) + acc[t, h] * (b / both)
        return mixed, top + jnp.log2(both)

    def emit(way, t, h, o, l):
        rout[t, h] = o.astype(jnp.bfloat16)
        lout[t, h] = l
        for copy in r_copies(way, t, h):
            copy.start()

    @pl.loop(0, heads)
    def _(h):
        qbuf[me, h] = q_ref[h]

    to_right = 2 * me < n - 1
    shorter = jnp.where(to_right, me, n - 1 - me)
    sign = jnp.where(to_right, 1, -1)
    near_way = jnp.where(to_right, 0, 1)

    def tile_of(k):
        paired = k <= 2 * shorter
        distance = jnp.where(paired, (k + 1) // 2, k - shorter)
        side = jnp.where(paired & (k % 2 == 0), -sign, sign)
        return jnp.where(k == n, me, me + side * distance)

    def chain(way, r, h):
        t = jnp.where(way == 0, r, n - 1 - r)
        inner = jnp.where(way == 0, (me > 0) & (me < t), (me < n - 1) & (me > t))

        @pl.when(inner)
        def _():
            for copy in r_copies(way, t, h):
                copy.wait_recv()
            o, l = merge(way, t, h)
            emit(way, t, h, o, l)

    @pl.loop(0, n * heads + 2)
    def _(u):
        k, h = u // heads + 1, u % heads

        for way in (0, 1):
            t = me - k if way == 0 else me + k

            @pl.when((t >= 0) & (t < n) & (k < n))
            def _():
                q_copy(qbuf.at[t, h], way, t, h).wait_recv()

                @pl.when(can_send(way))
                def _():
                    q_copy(qbuf.at[t, h], way, t, h).start()

        @pl.when(k <= n)
        def _():
            t = tile_of(k)
            o, l = partial(qbuf[t, h], t, h)
            first = ((me == 0) | (me == n - 1)) & (k < n)

            @pl.when(jnp.logical_not(first))
            def _():
                acc[t, h] = o
                lacc[t, h] = l

            @pl.when(first)
            def _():
                emit(near_way, t, h, o, l)

        for way, lag in ((near_way, heads), (1 - near_way, heads + 1)):
            v = u - lag

            @pl.when((v >= 0) & (v < (n - 1) * heads))
            def _():
                chain(way, v // heads + 1, v % heads)

        e = u - (n - 1) * heads - 2

        @pl.when(e >= 0)
        def _():
            for way in (0, 1):
                @pl.when(can_send(1 - way))
                def _():
                    for copy in r_copies(way, me, e):
                        copy.wait_recv()
                    o, l = merge(way, me, e)
                    acc[me, e] = o
                    lacc[me, e] = l
            out_ref[e] = acc[me, e].T.astype(out_ref.dtype)

    @pl.loop(0, heads)
    def _(h):
        for way in (0, 1):
            @pl.when(can_send(way))
            def _():
                q_copy(q_ref.at[h], way, me, h).wait_send()

        @pl.loop(0, n)
        def _(t):
            @pl.when(t != me)
            def _():
                for copy in r_copies(0, t, h):
                    copy.wait_send()

            @pl.when((t < me) & can_send(0))
            def _():
                q_copy(qbuf.at[t, h], 0, t, h).wait_send()

            @pl.when((t > me) & can_send(1))
            def _():
                q_copy(qbuf.at[t, h], 1, t, h).wait_send()


def shards(
    n, queries, new_keys, new_values, cache_keys, cache_values, block_slot, block_lists, frame_pos
):
    tok, heads, hd = queries.shape[1:]
    kv_heads = new_keys.shape[2]
    cb_dev = cache_keys.shape[1] // BLOCK
    capacity = min(cb_dev, max(2, -(-block_lists.shape[3] // n)))
    slots, limits = local_blocks(
        block_slot[0], block_lists[0], frame_pos[0], lax.axis_index("ctx"), cb_dev, capacity
    )
    q = jnp.transpose(queries[0], (1, 0, 2))
    kn = jnp.transpose(new_keys[0], (1, 0, 2))
    vn = jnp.transpose(new_values[0], (1, 2, 0))
    kc = jnp.transpose(cache_keys[0].reshape(cb_dev, BLOCK, kv_heads, hd), (2, 0, 1, 3))
    vc = jnp.transpose(cache_values[0].reshape(cb_dev, BLOCK, kv_heads, hd), (2, 0, 3, 1))
    smem = pl.BlockSpec(memory_space=pltpu.SMEM)
    vmem = pl.BlockSpec(memory_space=pltpu.VMEM)
    bf16, f32 = jnp.bfloat16, jnp.float32
    dma = pltpu.SemaphoreType.DMA
    out = pl.pallas_call(
        functools.partial(kernel, n),
        out_shape=jax.ShapeDtypeStruct((heads, tok, hd), bf16),
        in_specs=[smem, smem] + [vmem] * 5,
        out_specs=vmem,
        scratch_shapes=[
            pltpu.VMEM((n, heads, tok, hd), bf16),
            pltpu.VMEM((2, n, heads, hd, tok), bf16),
            pltpu.VMEM((2, n, heads, 1, tok), f32),
            pltpu.VMEM((n, heads, hd, tok), bf16),
            pltpu.VMEM((n, heads, 1, tok), f32),
            pltpu.VMEM((n, heads, hd, tok), f32),
            pltpu.VMEM((n, heads, 1, tok), f32),
            dma((2, n, heads)),
            dma((n, heads)),
            dma((n, heads)),
            dma((2, n, heads)),
            dma((n, heads)),
            dma((2, n, heads)),
        ],
        compiler_params=pltpu.CompilerParams(
            collective_id=0, has_side_effects=True, vmem_limit_bytes=56 * 1024 * 1024
        ),
    )(slots, limits, q, kn, vn, kc, vc)
    return jnp.transpose(out, (1, 0, 2))[None]


def solution(mesh):
    placed = (
        P(("groups", "stream"), "ctx", "head", None),
        P(("groups", "stream"), "ctx", "head", None),
        P(("groups", "stream"), "ctx", "head", None),
        P(("groups", "stream"), "ctx", "head", None),
        P(("groups", "stream"), "ctx", "head", None),
        P(("groups", "stream"), None),
        P(("groups", "stream"), "head", None, None),
        P(("groups", "stream")),
    )
    return jax.shard_map(
        functools.partial(shards, mesh.shape["ctx"]),
        mesh=mesh,
        in_specs=placed,
        out_specs=P(("groups", "stream"), "ctx", "head", None),
        check_vma=False,
    )
```

```python
import functools

import jax
import jax.numpy as jnp
from jax import lax
from jax.experimental import pallas as pl
from jax.experimental.pallas import tpu as pltpu
from jax.sharding import PartitionSpec as P

BLOCK = 128
FLOOR = -1e30
LOG2E = 1.4426950408889634
MESH = pl.DeviceIdType.MESH


def lookup(slot_table, indices):
    entries = jnp.arange(slot_table.shape[0], dtype=jnp.int32)
    return jnp.sum(jnp.where(indices[..., None] == entries, slot_table, 0), axis=-1)


def local_blocks(slot_table, lists, filled, own_index, cb_dev, capacity):
    slot_entry = lookup(slot_table, lists)
    mine = (slot_entry // cb_dev) == own_index
    count = lists.shape[-1]
    positions = jnp.arange(count, dtype=jnp.int32)
    earlier = positions[:, None] > positions[None, :]
    rank = jnp.sum((mine[..., None, :] & earlier).astype(jnp.int32), axis=-1)
    slot_ids = jnp.arange(capacity, dtype=jnp.int32)
    matched = mine[..., None] & (rank[..., None] == slot_ids)
    rows = jnp.clip(filled - lists * BLOCK, 0, BLOCK)
    slots = jnp.sum(jnp.where(matched, (slot_entry % cb_dev)[..., None], 0), axis=2)
    limits = jnp.sum(jnp.where(matched, rows[..., None], 0), axis=2)
    return slots, limits


def kernel(
    n, slots_ref, limits_ref, q_ref, ql_ref, qr_ref, kn_ref, vn_ref, kc_ref, vc_ref, out_ref,
    qbuf, rin, lin, rout, lout, acc, lacc, qs, qr, rs, rr, ls, lr,
):
    heads, tok, hd = q_ref.shape
    group = heads // kn_ref.shape[0]
    capacity = slots_ref.shape[2]
    early = ql_ref.shape[0]
    me = lax.axis_index("ctx")
    scale = LOG2E * hd ** -0.5

    barrier = pltpu.get_barrier_semaphore()

    @pl.when(me > 0)
    def _():
        pl.semaphore_signal(barrier, inc=1, device_id={"ctx": me - 1}, device_id_type=MESH)

    @pl.when(me < n - 1)
    def _():
        pl.semaphore_signal(barrier, inc=1, device_id={"ctx": me + 1}, device_id_type=MESH)

    peers = jnp.where(me > 0, 1, 0) + jnp.where(me < n - 1, 1, 0)
    pl.semaphore_wait(barrier, peers)

    def q_copy(src, way, t, h):
        return pltpu.make_async_remote_copy(
            src_ref=src, dst_ref=qbuf.at[t, h], send_sem=qs.at[way, t, h], recv_sem=qr.at[t, h],
            device_id={"ctx": me + 1 - 2 * way}, device_id_type=MESH,
        )

    def r_copies(way, t, h):
        peer = {"ctx": me + 1 - 2 * way}
        return (
            pltpu.make_async_remote_copy(
                src_ref=rout.at[t, h], dst_ref=rin.at[way, t, h], send_sem=rs.at[t, h],
                recv_sem=rr.at[way, t, h], device_id=peer, device_id_type=MESH,
            ),
            pltpu.make_async_remote_copy(
                src_ref=lout.at[t, h], dst_ref=lin.at[way, t, h], send_sem=ls.at[t, h],
                recv_sem=lr.at[way, t, h], device_id=peer, device_id_type=MESH,
            ),
        )

    def can_send(way):
        return me < n - 1 if way == 0 else me > 0

    @pl.loop(early, heads)
    def _(h):
        for way in (0, 1):
            @pl.when(can_send(way))
            def _():
                q_copy(q_ref.at[h], way, me, h).start()

    def partial(q, t, h):
        g = h // group
        rows = lax.broadcasted_iota(jnp.int32, (BLOCK, tok), 0)
        nt = (((1,), (1,)), ((), ()))
        pieces = [
            ([lax.dot_general(kn_ref[g], q, nt, preferred_element_type=jnp.float32)], vn_ref[g])
        ]
        for first in range(0, capacity, 4):
            ids = range(first, min(first + 4, capacity))
            where = [slots_ref[g, t, c] for c in ids]
            keys = jnp.concatenate([kc_ref[g, w] for w in where], axis=0)
            values = jnp.concatenate([vc_ref[g, w] for w in where], axis=1)
            s = lax.dot_general(keys, q, nt, preferred_element_type=jnp.float32)
            parts = []
            for k, c in enumerate(ids):
                block = s[k * BLOCK:(k + 1) * BLOCK]
                parts.append(jnp.where(rows < limits_ref[g, t, c], block, FLOOR))
            pieces.append((parts, values))
        peak = None
        for parts, _ in pieces:
            for s in parts:
                top = jnp.max(s, axis=0, keepdims=True)
                peak = top if peak is None else jnp.maximum(peak, top)
        peak = peak * scale
        total = jnp.zeros((1, tok), jnp.float32)
        running = jnp.zeros((hd, tok), jnp.float32)
        for parts, values in pieces:
            weights = []
            for s in parts:
                w = jnp.exp2(s * scale - peak)
                total = total + jnp.sum(w, axis=0, keepdims=True)
                weights.append(w.astype(jnp.bfloat16))
            p = weights[0] if len(weights) == 1 else jnp.concatenate(weights, axis=0)
            running = running + jnp.dot(values, p, preferred_element_type=jnp.float32)
        return running / total, peak + jnp.log2(total)

    def merge(way, t, h):
        theirs, ours = lin[way, t, h], lacc[t, h]
        top = jnp.maximum(theirs, ours)
        a, b = jnp.exp2(theirs - top), jnp.exp2(ours - top)
        both = a + b
        mixed = rin[way, t, h].astype(jnp.float32) * (a / both) + acc[t, h] * (b / both)
        return mixed, top + jnp.log2(both)

    def emit(way, t, h, o, l):
        rout[t, h] = o.astype(jnp.bfloat16)
        lout[t, h] = l
        for copy in r_copies(way, t, h):
            copy.start()

    @pl.loop(0, heads)
    def _(h):
        qbuf[me, h] = q_ref[h]

    @pl.loop(0, early)
    def _(h):
        @pl.when(me > 0)
        def _():
            qbuf[me - 1, h] = ql_ref[h]

        @pl.when(me < n - 1)
        def _():
            qbuf[me + 1, h] = qr_ref[h]

    to_right = 2 * me < n - 1
    shorter = jnp.where(to_right, me, n - 1 - me)
    sign = jnp.where(to_right, 1, -1)
    near_way = jnp.where(to_right, 0, 1)

    def tile_of(k):
        paired = k <= 2 * shorter
        distance = jnp.where(paired, (k + 1) // 2, k - shorter)
        side = jnp.where(paired & (k % 2 == 0), -sign, sign)
        return jnp.where(k == n, me, me + side * distance)

    def chain(way, r, h):
        t = jnp.where(way == 0, r, n - 1 - r)
        inner = jnp.where(way == 0, (me > 0) & (me < t), (me < n - 1) & (me > t))

        @pl.when(inner)
        def _():
            for copy in r_copies(way, t, h):
                copy.wait_recv()
            o, l = merge(way, t, h)
            emit(way, t, h, o, l)

    @pl.loop(0, n * heads + 2)
    def _(u):
        k, h = u // heads + 1, u % heads

        for way in (0, 1):
            t = me - k if way == 0 else me + k

            @pl.when((t >= 0) & (t < n) & (k < n))
            def _():
                @pl.when((k > 1) | (h >= early))
                def _():
                    q_copy(qbuf.at[t, h], way, t, h).wait_recv()

                @pl.when(can_send(way))
                def _():
                    q_copy(qbuf.at[t, h], way, t, h).start()

        @pl.when(k <= n)
        def _():
            t = tile_of(k)
            o, l = partial(qbuf[t, h], t, h)
            first = ((me == 0) | (me == n - 1)) & (k < n)

            @pl.when(jnp.logical_not(first))
            def _():
                acc[t, h] = o
                lacc[t, h] = l

            @pl.when(first)
            def _():
                emit(near_way, t, h, o, l)

        for way, lag in ((near_way, heads), (1 - near_way, heads + 1)):
            v = u - lag

            @pl.when((v >= 0) & (v < (n - 1) * heads))
            def _():
                chain(way, v // heads + 1, v % heads)

        e = u - (n - 1) * heads - 2

        @pl.when(e >= 0)
        def _():
            for way in (0, 1):
                @pl.when(can_send(1 - way))
                def _():
                    for copy in r_copies(way, me, e):
                        copy.wait_recv()
                    o, l = merge(way, me, e)
                    acc[me, e] = o
                    lacc[me, e] = l
            out_ref[e] = acc[me, e].T.astype(out_ref.dtype)

    @pl.loop(0, heads)
    def _(h):
        for way in (0, 1):
            @pl.when(can_send(way) & (h >= early))
            def _():
                q_copy(q_ref.at[h], way, me, h).wait_send()

        @pl.loop(0, n)
        def _(t):
            @pl.when(t != me)
            def _():
                for copy in r_copies(0, t, h):
                    copy.wait_send()

            @pl.when((t < me) & can_send(0))
            def _():
                q_copy(qbuf.at[t, h], 0, t, h).wait_send()

            @pl.when((t > me) & can_send(1))
            def _():
                q_copy(qbuf.at[t, h], 1, t, h).wait_send()


def shards(
    n, queries, new_keys, new_values, cache_keys, cache_values, block_slot, block_lists, frame_pos
):
    tok, heads, hd = queries.shape[1:]
    kv_heads = new_keys.shape[2]
    cb_dev = cache_keys.shape[1] // BLOCK
    capacity = min(cb_dev, max(2, -(-block_lists.shape[3] // n)))
    slots, limits = local_blocks(
        block_slot[0], block_lists[0], frame_pos[0], lax.axis_index("ctx"), cb_dev, capacity
    )
    q = jnp.transpose(queries[0], (1, 0, 2))
    early = heads // 2
    rights = [(i, i + 1) for i in range(n - 1)]
    q_left = lax.ppermute(q[:early], "ctx", rights)
    q_right = lax.ppermute(q[:early], "ctx", [(b, a) for a, b in rights])
    kn = jnp.transpose(new_keys[0], (1, 0, 2))
    vn = jnp.transpose(new_values[0], (1, 2, 0))
    kc = jnp.transpose(cache_keys[0].reshape(cb_dev, BLOCK, kv_heads, hd), (2, 0, 1, 3))
    vc = jnp.transpose(cache_values[0].reshape(cb_dev, BLOCK, kv_heads, hd), (2, 0, 3, 1))
    smem = pl.BlockSpec(memory_space=pltpu.SMEM)
    vmem = pl.BlockSpec(memory_space=pltpu.VMEM)
    bf16, f32 = jnp.bfloat16, jnp.float32
    dma = pltpu.SemaphoreType.DMA
    out = pl.pallas_call(
        functools.partial(kernel, n),
        out_shape=jax.ShapeDtypeStruct((heads, tok, hd), bf16),
        in_specs=[smem, smem] + [vmem] * 7,
        out_specs=vmem,
        scratch_shapes=[
            pltpu.VMEM((n, heads, tok, hd), bf16),
            pltpu.VMEM((2, n, heads, hd, tok), bf16),
            pltpu.VMEM((2, n, heads, 1, tok), f32),
            pltpu.VMEM((n, heads, hd, tok), bf16),
            pltpu.VMEM((n, heads, 1, tok), f32),
            pltpu.VMEM((n, heads, hd, tok), f32),
            pltpu.VMEM((n, heads, 1, tok), f32),
            dma((2, n, heads)),
            dma((n, heads)),
            dma((n, heads)),
            dma((2, n, heads)),
            dma((n, heads)),
            dma((2, n, heads)),
        ],
        compiler_params=pltpu.CompilerParams(
            collective_id=0, has_side_effects=True, vmem_limit_bytes=56 * 1024 * 1024
        ),
    )(slots, limits, q, q_left, q_right, kn, vn, kc, vc)
    return jnp.transpose(out, (1, 0, 2))[None]


def solution(mesh):
    placed = (
        P(("groups", "stream"), "ctx", "head", None),
        P(("groups", "stream"), "ctx", "head", None),
        P(("groups", "stream"), "ctx", "head", None),
        P(("groups", "stream"), "ctx", "head", None),
        P(("groups", "stream"), "ctx", "head", None),
        P(("groups", "stream"), None),
        P(("groups", "stream"), "head", None, None),
        P(("groups", "stream")),
    )
    return jax.shard_map(
        functools.partial(shards, mesh.shape["ctx"]),
        mesh=mesh,
        in_specs=placed,
        out_specs=P(("groups", "stream"), "ctx", "head", None),
        check_vma=False,
    )
```

```python
import functools

import jax
import jax.numpy as jnp
from jax import lax
from jax.experimental import pallas as pl
from jax.experimental.pallas import tpu as pltpu
from jax.sharding import PartitionSpec as P

BLOCK = 128
FLOOR = -1e30
LOG2E = 1.4426950408889634
MESH = pl.DeviceIdType.MESH


def lookup(slot_table, indices):
    entries = jnp.arange(slot_table.shape[0], dtype=jnp.int32)
    return jnp.sum(jnp.where(indices[..., None] == entries, slot_table, 0), axis=-1)


def local_blocks(slot_table, lists, filled, own_index, cb_dev, capacity):
    slot_entry = lookup(slot_table, lists)
    mine = (slot_entry // cb_dev) == own_index
    count = lists.shape[-1]
    positions = jnp.arange(count, dtype=jnp.int32)
    earlier = positions[:, None] > positions[None, :]
    rank = jnp.sum((mine[..., None, :] & earlier).astype(jnp.int32), axis=-1)
    slot_ids = jnp.arange(capacity, dtype=jnp.int32)
    matched = mine[..., None] & (rank[..., None] == slot_ids)
    rows = jnp.clip(filled - lists * BLOCK, 0, BLOCK)
    slots = jnp.sum(jnp.where(matched, (slot_entry % cb_dev)[..., None], 0), axis=2)
    limits = jnp.sum(jnp.where(matched, rows[..., None], 0), axis=2)
    return slots, limits


def kernel(
    n, slots_ref, limits_ref, q_ref, ql_ref, qr_ref, kn_ref, vn_ref, kc_ref, vc_ref, out_ref,
    qbuf, rin, lin, rout, lout, acc, lacc, qs, qr, rs, rr, ls, lr,
):
    heads, tok, hd = q_ref.shape
    group = heads // kn_ref.shape[0]
    capacity = slots_ref.shape[2]
    early = ql_ref.shape[0]
    me = lax.axis_index("ctx")
    scale = LOG2E * hd ** -0.5

    barrier = pltpu.get_barrier_semaphore()

    @pl.when(me > 0)
    def _():
        pl.semaphore_signal(barrier, inc=1, device_id={"ctx": me - 1}, device_id_type=MESH)

    @pl.when(me < n - 1)
    def _():
        pl.semaphore_signal(barrier, inc=1, device_id={"ctx": me + 1}, device_id_type=MESH)

    peers = jnp.where(me > 0, 1, 0) + jnp.where(me < n - 1, 1, 0)
    pl.semaphore_wait(barrier, peers)

    def q_copy(src, way, t, h):
        return pltpu.make_async_remote_copy(
            src_ref=src, dst_ref=qbuf.at[t, h], send_sem=qs.at[way, t, h], recv_sem=qr.at[t, h],
            device_id={"ctx": me + 1 - 2 * way}, device_id_type=MESH,
        )

    def r_copies(way, t, h):
        peer = {"ctx": me + 1 - 2 * way}
        return (
            pltpu.make_async_remote_copy(
                src_ref=rout.at[t, h], dst_ref=rin.at[way, t, h], send_sem=rs.at[t, h],
                recv_sem=rr.at[way, t, h], device_id=peer, device_id_type=MESH,
            ),
            pltpu.make_async_remote_copy(
                src_ref=lout.at[t, h], dst_ref=lin.at[way, t, h], send_sem=ls.at[t, h],
                recv_sem=lr.at[way, t, h], device_id=peer, device_id_type=MESH,
            ),
        )

    def can_send(way):
        return me < n - 1 if way == 0 else me > 0

    def partial(q, t, h):
        g = h // group
        rows = lax.broadcasted_iota(jnp.int32, (BLOCK, tok), 0)
        nt = (((1,), (1,)), ((), ()))
        pieces = [
            ([lax.dot_general(kn_ref[g], q, nt, preferred_element_type=jnp.float32)], vn_ref[g])
        ]
        for first in range(0, capacity, 4):
            ids = range(first, min(first + 4, capacity))
            where = [slots_ref[g, t, c] for c in ids]
            keys = jnp.concatenate([kc_ref[g, w] for w in where], axis=0)
            values = jnp.concatenate([vc_ref[g, w] for w in where], axis=1)
            s = lax.dot_general(keys, q, nt, preferred_element_type=jnp.float32)
            parts = []
            for k, c in enumerate(ids):
                block = s[k * BLOCK:(k + 1) * BLOCK]
                parts.append(jnp.where(rows < limits_ref[g, t, c], block, FLOOR))
            pieces.append((parts, values))
        peak = None
        for parts, _ in pieces:
            for s in parts:
                top = jnp.max(s, axis=0, keepdims=True)
                peak = top if peak is None else jnp.maximum(peak, top)
        peak = peak * scale
        total = jnp.zeros((1, tok), jnp.float32)
        running = jnp.zeros((hd, tok), jnp.float32)
        for parts, values in pieces:
            weights = []
            for s in parts:
                w = jnp.exp2(s * scale - peak)
                total = total + jnp.sum(w, axis=0, keepdims=True)
                weights.append(w.astype(jnp.bfloat16))
            p = weights[0] if len(weights) == 1 else jnp.concatenate(weights, axis=0)
            running = running + jnp.dot(values, p, preferred_element_type=jnp.float32)
        return running / total, peak + jnp.log2(total)

    def merge(way, t, h):
        theirs, ours = lin[way, t, h], lacc[t, h]
        top = jnp.maximum(theirs, ours)
        a, b = jnp.exp2(theirs - top), jnp.exp2(ours - top)
        both = a + b
        mixed = rin[way, t, h].astype(jnp.float32) * (a / both) + acc[t, h] * (b / both)
        return mixed, top + jnp.log2(both)

    def emit(way, t, h, o, l):
        rout[t, h] = o.astype(jnp.bfloat16)
        lout[t, h] = l
        for copy in r_copies(way, t, h):
            copy.start()

    @pl.loop(0, early)
    def _(h):
        @pl.when(me > 0)
        def _():
            qbuf[me - 1, h] = ql_ref[h]

            @pl.when(can_send(0))
            def _():
                q_copy(qbuf.at[me - 1, h], 0, me - 1, h).start()

        @pl.when(me < n - 1)
        def _():
            qbuf[me + 1, h] = qr_ref[h]

            @pl.when(can_send(1))
            def _():
                q_copy(qbuf.at[me + 1, h], 1, me + 1, h).start()

    @pl.loop(early, heads)
    def _(h):
        for way in (0, 1):
            @pl.when(can_send(way))
            def _():
                q_copy(q_ref.at[h], way, me, h).start()

    @pl.loop(0, heads)
    def _(h):
        qbuf[me, h] = q_ref[h]

    to_right = 2 * me < n - 1
    shorter = jnp.where(to_right, me, n - 1 - me)
    sign = jnp.where(to_right, 1, -1)
    near_way = jnp.where(to_right, 0, 1)

    def tile_of(k):
        paired = k <= 2 * shorter
        distance = jnp.where(paired, (k + 1) // 2, k - shorter)
        side = jnp.where(paired & (k % 2 == 0), -sign, sign)
        return jnp.where(k == n, me, me + side * distance)

    def chain(way, r, h):
        t = jnp.where(way == 0, r, n - 1 - r)
        inner = jnp.where(way == 0, (me > 0) & (me < t), (me < n - 1) & (me > t))

        @pl.when(inner)
        def _():
            for copy in r_copies(way, t, h):
                copy.wait_recv()
            o, l = merge(way, t, h)
            emit(way, t, h, o, l)

    @pl.loop(0, n * heads + 2)
    def _(u):
        k, h = u // heads + 1, u % heads

        for way in (0, 1):
            t = me - k if way == 0 else me + k

            @pl.when((t >= 0) & (t < n) & (k < n) & ((k > 1) | (h >= early)))
            def _():
                q_copy(qbuf.at[t, h], way, t, h).wait_recv()

                @pl.when(can_send(way))
                def _():
                    q_copy(qbuf.at[t, h], way, t, h).start()

        for way, lag in ((near_way, heads), (1 - near_way, heads + 1)):
            v = u - lag

            @pl.when((v >= 0) & (v < (n - 1) * heads))
            def _():
                chain(way, v // heads + 1, v % heads)

        @pl.when(k <= n)
        def _():
            t = tile_of(k)
            o, l = partial(qbuf[t, h], t, h)
            first = ((me == 0) | (me == n - 1)) & (k < n)

            @pl.when(jnp.logical_not(first))
            def _():
                acc[t, h] = o
                lacc[t, h] = l

            @pl.when(first)
            def _():
                emit(near_way, t, h, o, l)

        e = u - (n - 1) * heads - 2

        @pl.when(e >= 0)
        def _():
            for way in (0, 1):
                @pl.when(can_send(1 - way))
                def _():
                    for copy in r_copies(way, me, e):
                        copy.wait_recv()
                    o, l = merge(way, me, e)
                    acc[me, e] = o
                    lacc[me, e] = l
            out_ref[e] = acc[me, e].T.astype(out_ref.dtype)

    @pl.loop(0, heads)
    def _(h):
        for way in (0, 1):
            @pl.when(can_send(way) & (h >= early))
            def _():
                q_copy(q_ref.at[h], way, me, h).wait_send()

        @pl.loop(0, n)
        def _(t):
            @pl.when(t != me)
            def _():
                for copy in r_copies(0, t, h):
                    copy.wait_send()

            @pl.when((t < me) & can_send(0))
            def _():
                q_copy(qbuf.at[t, h], 0, t, h).wait_send()

            @pl.when((t > me) & can_send(1))
            def _():
                q_copy(qbuf.at[t, h], 1, t, h).wait_send()


def shards(
    n, queries, new_keys, new_values, cache_keys, cache_values, block_slot, block_lists, frame_pos
):
    tok, heads, hd = queries.shape[1:]
    kv_heads = new_keys.shape[2]
    cb_dev = cache_keys.shape[1] // BLOCK
    capacity = min(cb_dev, max(2, -(-block_lists.shape[3] // n)))
    slots, limits = local_blocks(
        block_slot[0], block_lists[0], frame_pos[0], lax.axis_index("ctx"), cb_dev, capacity
    )
    q = jnp.transpose(queries[0], (1, 0, 2))
    early = heads // 2
    rights = [(i, i + 1) for i in range(n - 1)]
    q_left = lax.ppermute(q[:early], "ctx", rights)
    q_right = lax.ppermute(q[:early], "ctx", [(b, a) for a, b in rights])
    kn = jnp.transpose(new_keys[0], (1, 0, 2))
    vn = jnp.transpose(new_values[0], (1, 2, 0))
    kc = jnp.transpose(cache_keys[0].reshape(cb_dev, BLOCK, kv_heads, hd), (2, 0, 1, 3))
    vc = jnp.transpose(cache_values[0].reshape(cb_dev, BLOCK, kv_heads, hd), (2, 0, 3, 1))
    smem = pl.BlockSpec(memory_space=pltpu.SMEM)
    vmem = pl.BlockSpec(memory_space=pltpu.VMEM)
    bf16, f32 = jnp.bfloat16, jnp.float32
    dma = pltpu.SemaphoreType.DMA
    out = pl.pallas_call(
        functools.partial(kernel, n),
        out_shape=jax.ShapeDtypeStruct((heads, tok, hd), bf16),
        in_specs=[smem, smem] + [vmem] * 7,
        out_specs=vmem,
        scratch_shapes=[
            pltpu.VMEM((n, heads, tok, hd), bf16),
            pltpu.VMEM((2, n, heads, hd, tok), bf16),
            pltpu.VMEM((2, n, heads, 1, tok), f32),
            pltpu.VMEM((n, heads, hd, tok), bf16),
            pltpu.VMEM((n, heads, 1, tok), f32),
            pltpu.VMEM((n, heads, hd, tok), f32),
            pltpu.VMEM((n, heads, 1, tok), f32),
            dma((2, n, heads)),
            dma((n, heads)),
            dma((n, heads)),
            dma((2, n, heads)),
            dma((n, heads)),
            dma((2, n, heads)),
        ],
        compiler_params=pltpu.CompilerParams(
            collective_id=0, has_side_effects=True, vmem_limit_bytes=56 * 1024 * 1024
        ),
    )(slots, limits, q, q_left, q_right, kn, vn, kc, vc)
    return jnp.transpose(out, (1, 0, 2))[None]


def solution(mesh):
    placed = (
        P(("groups", "stream"), "ctx", "head", None),
        P(("groups", "stream"), "ctx", "head", None),
        P(("groups", "stream"), "ctx", "head", None),
        P(("groups", "stream"), "ctx", "head", None),
        P(("groups", "stream"), "ctx", "head", None),
        P(("groups", "stream"), None),
        P(("groups", "stream"), "head", None, None),
        P(("groups", "stream")),
    )
    return jax.shard_map(
        functools.partial(shards, mesh.shape["ctx"]),
        mesh=mesh,
        in_specs=placed,
        out_specs=P(("groups", "stream"), "ctx", "head", None),
        check_vma=False,
    )
```
